128 devices in a mesh: row: 32 (over y, x, core), col: 4 (over z).
Axes of the slice: x: 4, y: 4, z: 4, core: 2. Of those that a mesh axis runs over, the one named last changes fastest.
Arguments:
- momentum: bfloat16 [16384, 26624], P(('row', 'col')), may hold values from -18 to 18
- gradient: bfloat16 [16384, 26624], P(('row', 'col')), may hold values from -9 to 9
- right_factor: bfloat16 [512, 26624], P('row', 'col'), may hold values from -0.0390625 to 0.0390625
Outputs:
- new_momentum: bfloat16 [16384, 26624], P('row', 'col')
- left_factor: float32 [16384, 512], P(('row', 'col'))
- new_right: float32 [512, 26624], P('row', 'col')
The draws below stay inside these ranges and needn't reach their ends.
All inputs are finite; a program needn't handle non-finite values.
Results may differ from the reference program's by a relative error of at most 0.017.
Values may be sent and summed in bfloat16 or wider, within the bound.
No kernel may reach another device: no remote copies, remote signals or barrier semaphores. Data moves between devices by JAX's collectives and lax.ppermute only.
A program may use at most 128 MiB of HBM per device.

```python
import jax
import jax.numpy as jnp
from jax import lax

D = 16384
FF = 26624
R = 512


def column_profile(top_scale):
    position = jnp.arange(FF, dtype=jnp.float32) / float(FF)
    return jnp.exp(position * jnp.log(jnp.float32(top_scale)))


def draw_field(key, base_scale):
    values = jax.random.truncated_normal(key, -6.0, 6.0, (D, FF), jnp.float32)
    return values * (base_scale * column_profile(3.0))[None, :]


def draw_momentum(key, part):
    key = jax.random.fold_in(key, 11)
    return draw_field(key, 1.0).astype(jnp.bfloat16)


def draw_gradient(key, part):
    key = jax.random.fold_in(key, 23)
    return draw_field(key, 0.5).astype(jnp.bfloat16)


def block_scale(stream_key, extent, shards, least, largest):
    def one(axis_at, blocks):
        heights = jax.random.uniform(jax.random.fold_in(jax.random.fold_in(stream_key, 6), axis_at), (blocks,), jnp.float32, least / len(shards), largest / len(shards))
        return jnp.repeat(jnp.exp(heights), extent[axis_at] // blocks).reshape((-1,) + (1,) * (len(extent) - axis_at - 1))

    gain = one(*shards[0])
    for cut in shards[1:]:
        gain = gain * one(*cut)
    return gain


def centred(own_key, extent, scale, most, pieces=(), kind=jnp.bfloat16):
    level = block_scale(own_key, extent, pieces, -0.22, 0.18) if pieces else 1.0
    result = jax.random.normal(own_key, extent, jnp.float32) * scale * level
    return jnp.minimum(jnp.maximum(result, -most), most).astype(kind)


def setup_inputs(seed: int = 0) -> dict:
    arg_keys = jax.random.split(jax.random.key(seed), 4)
    momentum = draw_momentum(jax.random.fold_in(arg_keys[3], 71), 0)
    gradient = draw_gradient(jax.random.fold_in(arg_keys[3], 71), 0)
    right_factor = centred(arg_keys[2], (R, FF), FF ** -0.5, 0.0390625, ((0, 32), (1, 4)))
    return {"momentum": momentum, "gradient": gradient, "right_factor": right_factor}


def orthonormalize(projected, gram_total):
    lower = jnp.linalg.cholesky(gram_total)
    identity = jnp.eye(gram_total.shape[0], dtype=gram_total.dtype)
    inverse = jax.scipy.linalg.solve_triangular(lower, identity, lower=True)
    return jnp.dot(projected, inverse.T, precision=lax.Precision.HIGHEST)

def reference(momentum, gradient, right_factor):
    blend = (momentum.astype(jnp.float32) + gradient.astype(jnp.float32)).astype(jnp.bfloat16)
    projected = lax.dot_general(blend.astype(jnp.float32), right_factor.astype(jnp.float32), (((1,), (1,)), ((), ())), preferred_element_type=jnp.float32)
    gram_total = jnp.dot(projected.T, projected, precision=lax.Precision.HIGHEST)
    orthonormal = orthonormalize(projected, gram_total)
    orth_half = orthonormal.astype(jnp.bfloat16)
    right_raw = lax.dot_general(orth_half.astype(jnp.float32), blend.astype(jnp.float32), (((0,), (0,)), ((), ())), preferred_element_type=jnp.float32)
    squares = lax.optimization_barrier(jnp.sum(right_raw * right_raw, axis=1))
    new_right = right_raw / jnp.sqrt(squares + 1e-06)[:, None]
    right_half = right_raw.astype(jnp.bfloat16)
    feedback = jnp.dot(orth_half.astype(jnp.float32), right_half.astype(jnp.float32), preferred_element_type=jnp.float32)
    new_momentum = (blend.astype(jnp.float32) - 0.75 * feedback).astype(jnp.bfloat16)
    left_factor = orthonormal * math_sqrt(D)
    return (new_momentum, left_factor, new_right)

def math_sqrt(value):
    return float(value) ** 0.5
```

```python
import jax
import jax.numpy as jnp
from jax import lax
from jax.experimental import pallas as pl
from jax.experimental.pallas import tpu as pltpu
from jax.sharding import PartitionSpec as P

D = 16384
HI=lax.Precision.HIGHEST
B=128
PANEL=8

def diagonal_inverse(a_ref, x_ref):
    row = lax.broadcasted_iota(jnp.int32, (B, B), 0)
    col = lax.broadcasted_iota(jnp.int32, (B, B), 1)
    x_ref[...] = jnp.where(row == col, 1.0, 0.0)
    panels = B // PANEL
    full = (PANEL, B)
    for p in range(panels):
        at = p * PANEL
        mine = a_ref[at:at + PANEL, :]
        xmine = x_ref[at:at + PANEL, :]
        cols = [jnp.broadcast_to(mine[:, at + j:at + j + 1], full) for j in range(PANEL)]
        a = {(i, j): jnp.broadcast_to(cols[j][i:i + 1, :], full) for j in range(PANEL) for i in range(j, PANEL)}
        inv = []
        for k in range(PANEL):
            inv.append(lax.rsqrt(a[k, k]))
            for i in range(k + 1, PANEL):
                a[i, k] = a[i, k] * inv[k]
            for j in range(k + 1, PANEL):
                for i in range(j, PANEL):
                    a[i, j] = a[i, j] - a[i, k] * a[j, k]
        def forward(block):
            y = []
            for i in range(PANEL):
                r = jnp.broadcast_to(block[i:i + 1, :], full)
                for j in range(i):
                    r = r - a[i, j] * y[j]
                y.append(r * inv[i])
            return y
        def backward(y):
            z = [None] * PANEL
            for i in range(PANEL - 1, -1, -1):
                r = y[i]
                for j in range(i + 1, PANEL):
                    r = r - a[j, i] * z[j]
                z[i] = r * inv[i]
            return z
        yx = forward(xmine)
        sub = lax.broadcasted_iota(jnp.int32, full, 0)
        out = yx[0]
        for i in range(1, PANEL):
            out = jnp.where(sub == i, yx[i], out)
        x_ref[at:at + PANEL, :] = out
        if p + 1 < panels:
            za = backward(forward(mine))
            zx = backward(yx)
            for q in range(p + 1, panels):
                s = slice(q * PANEL, (q + 1) * PANEL)
                block = a_ref[s, :]
                da = 0.0
                dx = 0.0
                for j in range(PANEL):
                    m = jnp.broadcast_to(block[:, at + j:at + j + 1], full)
                    da = da + m * za[j]
                    dx = dx + m * zx[j]
                a_ref[s, :] = block - da
                x_ref[s, :] = x_ref[s, :] - dx

def chol_kernel(g_ref, x_ref, a_s, d_s, i_s):
    n = g_ref.shape[0]
    nb = n // B
    a_s[...] = g_ref[...].astype(jnp.float32)
    x_ref[...] = jnp.zeros_like(x_ref)
    def dot(u, v, dims):
        return lax.dot_general(u, v, (dims, ((), ())), precision=HI, preferred_element_type=jnp.float32)
    def step(b, _):
        at = pl.multiple_of(b * B, B)
        here = pl.ds(at, B)
        d_s[...] = a_s[here, here]
        diagonal_inverse(d_s, i_s)
        inv = i_s[...]
        x_ref[here, here] = inv
        left = dot(inv, x_ref[here, :], ((1,), (0,)))
        lane = lax.broadcasted_iota(jnp.int32, (B, n), 1)
        own = (lane >= at) & (lane < at + B)
        wide = jnp.concatenate([inv] * nb, axis=1)
        y_x = jnp.where(own, wide, left)
        x_ref[here, :] = y_x
        @pl.when(b < nb - 1)
        def _():
            y_a = dot(inv, a_s[here, :], ((1,), (0,)))
            y_a = jnp.where(lane >= at + B, y_a, 0.0)
            a_s[...] = a_s[...] - dot(y_a, y_a, ((0,), (0,)))
            x_ref[...] = x_ref[...] - dot(y_a, y_x, ((0,), (0,)))
        return 0
    lax.fori_loop(0, nb, step, 0)

def cholesky_inverse(gram):
    n = gram.shape[0]
    return pl.pallas_call(
        chol_kernel,
        out_shape=jax.ShapeDtypeStruct((n, n), jnp.float32),
        in_specs=[pl.BlockSpec(memory_space=pltpu.VMEM)],
        out_specs=pl.BlockSpec(memory_space=pltpu.VMEM),
        scratch_shapes=[pltpu.VMEM((n, n), jnp.float32), pltpu.VMEM((B, B), jnp.float32), pltpu.VMEM((B, B), jnp.float32)],
        compiler_params=pltpu.CompilerParams(vmem_limit_bytes=16 * 2**20),
        cost_estimate=pl.CostEstimate(flops=2 * 10**9, bytes_accessed=2 * 2**20, transcendentals=0),
        name="cholesky_inverse",
    )(gram)


def per_device(momentum, gradient, right_factor):
    f32, half = jnp.float32, jnp.bfloat16
    ranks_dev = right_factor.shape[0]
    rows = lax.axis_size("row")
    cols = lax.axis_size("col")
    right_all = lax.all_gather(right_factor, "row", axis=0, tiled=True)
    blend = (momentum.astype(f32) + gradient.astype(f32)).astype(half)
    regrouped = lax.all_to_all(blend, "col", split_axis=1, concat_axis=0, tiled=True)
    block_rows = regrouped.shape[0]
    share = block_rows // cols
    ranks = right_all.shape[0]
    partial = lax.dot_general(
        regrouped, right_all, (((1,), (1,)), ((), ())), preferred_element_type=f32
    ).astype(half)
    pieces = lax.all_to_all(partial, "col", split_axis=0, concat_axis=0, tiled=True)
    mine = jnp.sum(pieces.reshape(cols, share, ranks).astype(f32), axis=0).astype(half)
    projected = lax.all_gather(mine, "col", axis=0, tiled=True)
    cross = lax.dot_general(
        projected, regrouped, (((0,), (0,)), ((), ())), preferred_element_type=f32
    ).astype(half)
    cross_total = lax.psum(cross, "row")
    gram_part = lax.dot_general(
        projected, projected, (((0,), (0,)), ((), ())), preferred_element_type=f32
    ).astype(half)
    gram_pieces = lax.all_to_all(gram_part, "row", split_axis=0, concat_axis=0, tiled=True)
    gram_mine = jnp.sum(gram_pieces.reshape(rows, ranks // rows, ranks).astype(f32), axis=0)
    gram = lax.all_gather(gram_mine.astype(half), "row", axis=0, tiled=True).astype(f32)
    inverse = cholesky_inverse(gram)
    left_local = jnp.dot(mine.astype(f32), inverse.T, precision=HI)
    left_factor = left_local * float(D) ** 0.5
    orthonormal = jnp.dot(projected.astype(f32), inverse.T, precision=HI)
    weights = (0.75 * jnp.dot(orthonormal, inverse, precision=HI)).astype(half)
    own = lax.dynamic_slice_in_dim(inverse, lax.axis_index("row") * ranks_dev, ranks_dev, 0)
    high = own.astype(half)
    low = (own - high.astype(f32)).astype(half)
    both = jnp.dot(
        jnp.concatenate([high, low], axis=0), cross_total, preferred_element_type=f32
    )
    right_raw = both[:ranks_dev] + both[ranks_dev:]
    squares = lax.psum(jnp.sum(right_raw * right_raw, axis=1), "col")
    feedback = jnp.dot(weights, cross_total, preferred_element_type=f32)
    new_momentum = (regrouped.astype(f32) - feedback).astype(half)
    new_right = right_raw / jnp.sqrt(squares + 1e-06)[:, None]
    return (new_momentum, left_factor, new_right)


def solution(mesh):
    in_specs = (P(("row", "col"), None), P(("row", "col"), None), P("row", "col"))
    out_specs = (P("row", "col"), P(("row", "col"), None), P("row", "col"))
    return jax.shard_map(
        per_device, mesh=mesh, in_specs=in_specs, out_specs=out_specs, check_vma=False
    )
```

```python
import functools
import math

import jax
import jax.numpy as jnp
from jax import lax
from jax.experimental import pallas as pl
from jax.experimental.pallas import tpu as pltpu
from jax.sharding import Mesh, PartitionSpec as P

D = 16384
HI=lax.Precision.HIGHEST
B=128
PANEL=8

def total(terms):
    while len(terms) > 1:
        terms = [sum(terms[i:i + 2][1:], terms[i]) for i in range(0, len(terms), 2)]
    return terms[0]


def diagonal_inverse(a_ref, x_ref):
    row = lax.broadcasted_iota(jnp.int32, (B, B), 0)
    col = lax.broadcasted_iota(jnp.int32, (B, B), 1)
    x_ref[...] = jnp.where(row == col, 1.0, 0.0)
    panels = B // PANEL
    full = (PANEL, B)
    for p in range(panels):
        at = p * PANEL
        mine = a_ref[at:at + PANEL, :]
        xmine = x_ref[at:at + PANEL, :]
        cols = [jnp.broadcast_to(mine[:, at + j:at + j + 1], full) for j in range(PANEL)]
        a = {(i, j): jnp.broadcast_to(cols[j][i:i + 1, :], full) for j in range(PANEL) for i in range(j, PANEL)}
        low = {}
        for k in range(PANEL):
            root = lax.rsqrt(a[k, k])
            for i in range(k + 1, PANEL):
                a[i, k] = a[i, k] * root
            for j in range(k + 1, PANEL):
                for i in range(j, PANEL):
                    a[i, j] = a[i, j] - a[i, k] * a[j, k]
            for j in range(k):
                low[k, j] = -root * total([a[k, i] * low[i, j] for i in range(j, k)])
            low[k, k] = root

        def forward(block):
            r = [jnp.broadcast_to(block[i:i + 1, :], full) for i in range(PANEL)]
            return [total([low[i, j] * r[j] for j in range(i + 1)]) for i in range(PANEL)]

        def backward(y):
            return [total([low[j, i] * y[j] for j in range(i, PANEL)]) for i in range(PANEL)]

        yx = forward(xmine)
        sub = lax.broadcasted_iota(jnp.int32, full, 0)
        out = yx[0]
        for i in range(1, PANEL):
            out = jnp.where(sub == i, yx[i], out)
        x_ref[at:at + PANEL, :] = out
        if p + 1 < panels:
            za = backward(forward(mine))
            zx = backward(yx)
            for q in range(p + 1, panels):
                s = slice(q * PANEL, (q + 1) * PANEL)
                block = a_ref[s, :]
                m = [jnp.broadcast_to(block[:, at + j:at + j + 1], full) for j in range(PANEL)]
                a_ref[s, :] = block - total([m[j] * za[j] for j in range(PANEL)])
                x_ref[s, :] = x_ref[s, :] - total([m[j] * zx[j] for j in range(PANEL)])

def factor_kernel(at_ref, g_ref, *refs):
    factors, outs, scratch = refs[:4], refs[4:7], refs[7:]
    own_ref, weights_ref, left_ref, a_s, x_ref, d_s, i_s, sems = scratch
    copies = [
        pltpu.make_async_copy(ref, out, sems.at[i])
        for i, (ref, out) in enumerate(zip((own_ref, weights_ref, left_ref), outs))
    ]
    n = g_ref.shape[0]
    nb = n // B
    a_s[...] = g_ref[...].astype(jnp.float32)
    x_ref[...] = jnp.zeros_like(x_ref)

    def split(value):
        high = value.astype(jnp.bfloat16)
        return high, (value - high.astype(jnp.float32)).astype(jnp.bfloat16)

    def half_dot(u, v, dims):
        return lax.dot_general(u, v, (dims, ((), ())), preferred_element_type=jnp.float32)

    def dot(u, v, dims):
        (u_high, u_low), (v_high, v_low) = u, v
        return half_dot(u_high, v_high, dims) + (half_dot(u_high, v_low, dims) + half_dot(u_low, v_high, dims))

    def step(b, _):
        at = pl.multiple_of(b * B, B)
        here = pl.ds(at, B)
        d_s[...] = a_s[here, here]
        diagonal_inverse(d_s, i_s)
        for k in range(nb):
            @pl.when(b == k)
            def _(here=slice(k * B, (k + 1) * B), before=k * B, rest=slice((k + 1) * B, n)):
                inv = split(i_s[...])
                x_ref[here, here] = i_s[...]
                if before:
                    x_ref[here, :before] = dot(inv, split(x_ref[here, :before]), ((1,), (0,)))
                if rest.start < n:
                    y_x = split(x_ref[here, :here.stop])
                    y_a = split(dot(inv, split(a_s[here, rest]), ((1,), (0,))))
                    a_s[rest, rest] = a_s[rest, rest] - dot(y_a, y_a, ((0,), (0,)))
                    x_ref[rest, :here.stop] = x_ref[rest, :here.stop] - dot(y_a, y_x, ((0,), (0,)))
        return 0

    lax.fori_loop(0, nb, step, 0)

    count = own_ref.shape[0] // 2
    own = x_ref[pl.ds(pl.multiple_of(at_ref[0] * count, count), count), :]
    own_ref[:count, :], own_ref[count:, :] = split(own)
    copies[0].start()
    high, low = split(x_ref[...])
    factor = jnp.concatenate([f[...] for f in factors], axis=1)
    turned = half_dot(high, factor, ((1,), (0,))) + half_dot(low, factor, ((1,), (0,)))
    rows = left_ref.shape[0]
    left_ref[...] = turned[:, :rows].T * float(D) ** 0.5
    copies[2].start()
    turned_high, turned_low = split(turned)
    weights = half_dot(turned_high, high, ((0,), (0,)))
    weights += half_dot(turned_low, high, ((0,), (0,)))
    weights += half_dot(turned_high, low, ((0,), (0,)))
    weights_ref[...] = (0.75 * weights).astype(jnp.bfloat16)
    copies[1].start()
    for copy in copies:
        copy.wait()


def factorize(gram, factors, place, count):
    n = gram.shape[0]
    rows = factors[0].shape[1]
    vmem = pl.BlockSpec(memory_space=pltpu.VMEM)
    outs = [((2 * count, n), jnp.bfloat16), ((4 * rows, n), jnp.bfloat16), ((rows, n), jnp.float32)]
    return pl.pallas_call(
        factor_kernel,
        out_shape=[pltpu.HBM(*out) for out in outs],
        in_specs=[pl.BlockSpec(memory_space=pltpu.SMEM)] + [vmem] * 5,
        out_specs=[pl.BlockSpec(memory_space=pltpu.HBM)] * 3,
        scratch_shapes=[pltpu.VMEM(*out) for out in outs]
        + [pltpu.VMEM((n, n), jnp.float32)] * 2
        + [pltpu.VMEM((B, B), jnp.float32)] * 2
        + [pltpu.SemaphoreType.DMA((3,))],
        compiler_params=pltpu.CompilerParams(vmem_limit_bytes=16 * 2**20),
        cost_estimate=pl.CostEstimate(flops=2 * 10**10, bytes_accessed=4 * 2**20, transcendentals=0),
        name="factorize",
    )(jnp.full((1,), place, jnp.int32), gram, *factors)


TILE = 1664
CHUNK = 512
QUARTER = 128
EIGHTH = 32
F32 = jnp.float32
HALF = jnp.bfloat16
VMEM = pl.BlockSpec(memory_space=pltpu.VMEM)
SMEM = pl.BlockSpec(memory_space=pltpu.SMEM)
HBM = pl.BlockSpec(memory_space=pltpu.HBM)


def ring(value, axis, shift):
    size = lax.axis_size(axis)
    return lax.ppermute(value, axis, [(i, (i + shift) % size) for i in range(size)])


def swap_cores(value):
    return lax.ppermute(value, "core", [(0, 1), (1, 0)])


def in_hbm(values):
    return [pltpu.with_memory_space_constraint(value, pltpu.HBM) for value in values]


def call(kernel, name, operands, out_shape, scratch=(), in_specs=None, out_specs=None, flops=0):
    shapes = out_shape if isinstance(out_shape, list) else [out_shape]
    moved = sum(math.prod(v.shape) * v.dtype.itemsize for v in list(operands) + shapes)
    return pl.pallas_call(
        kernel,
        in_specs=in_specs or [VMEM] * len(operands),
        out_specs=out_specs or ([VMEM] * len(shapes) if isinstance(out_shape, list) else VMEM),
        out_shape=out_shape,
        scratch_shapes=list(scratch),
        compiler_params=pltpu.CompilerParams(vmem_limit_bytes=16 * 2**20),
        cost_estimate=pl.CostEstimate(flops=int(flops), bytes_accessed=int(moved), transcendentals=0),
        name=name,
    )(*operands)


def project_kernel(half, *refs):
    blocks, right = refs[:4], refs[4]
    rows, width = blocks[0].shape
    total = refs[5][...] if half else 0.0
    for at in range(0, width, TILE):
        block = jnp.concatenate([b[:, at:at + TILE] for b in blocks], axis=0)
        total += lax.dot_general(
            block,
            right[:, half * width + at:half * width + at + TILE],
            (((1,), (1,)), ((), ())),
            preferred_element_type=F32,
        )
    if half:
        for i, out in enumerate(refs[6:]):
            out[...] = total[i * rows:(i + 1) * rows].astype(HALF)
    else:
        refs[5][...] = total


def project(blocks, right, half, before=None):
    rows, width = blocks[0].shape
    ranks = right.shape[0]
    if half:
        out_shape = [jax.ShapeDtypeStruct((rows, ranks), HALF)] * 4
    else:
        out_shape = jax.ShapeDtypeStruct((4 * rows, ranks), F32)
    return call(
        functools.partial(project_kernel, half),
        "project",
        [*blocks, right] + ([before] if half else []),
        out_shape,
        flops=8 * rows * width * ranks,
    )


def settle_kernel(*refs):
    terms, out, turned = refs[:4], refs[4], refs[5]
    total = terms[0][...].astype(F32)
    for term in terms[1:]:
        total += term[...].astype(F32)
    out[...] = total.astype(HALF)
    turned[...] = total.T.astype(HALF)


def settle(terms):
    rows, ranks = terms[0].shape
    return call(
        settle_kernel,
        "settle",
        terms,
        [jax.ShapeDtypeStruct((rows, ranks), HALF), jax.ShapeDtypeStruct((ranks, rows), HALF)],
        flops=4 * rows * ranks,
    )


def gram_kernel(*refs):
    total = 0.0
    for factor in refs[:4]:
        total += lax.dot_general(
            factor[...], factor[...], (((1,), (1,)), ((), ())), preferred_element_type=F32
        )
    refs[4][...] = total.astype(HALF)


def gram_of(factors):
    ranks, rows = factors[0].shape
    return call(
        gram_kernel,
        "gram",
        factors,
        jax.ShapeDtypeStruct((ranks, ranks), HALF),
        flops=8 * rows * ranks * ranks,
    )


def spread_kernel(pieces_ref, out_ref):
    total = pieces_ref[0].astype(F32)
    for i in range(1, pieces_ref.shape[0]):
        total += pieces_ref[i].astype(F32)
    out_ref[...] = jnp.broadcast_to(total.astype(HALF)[None], out_ref.shape)


def spread(pieces):
    return call(spread_kernel, "spread", [pieces], jax.ShapeDtypeStruct(pieces.shape, HALF), flops=pieces.size)


def cross_kernel(half, adds, at_ref, *refs):
    factors, blocks = refs[:4], refs[4:8]
    extra = refs[8] if adds else None
    outs, (mixed, held, sems) = refs[8 + adds:-3], refs[-3:]
    rows = blocks[0].shape[0]
    base = pl.multiple_of(at_ref[0] * TILE, 128)
    copies = []
    for turn in range(4):
        quarter = lax.rem(at_ref[1] + turn, 4)
        for part in range(4):
            at = part * QUARTER + quarter * EIGHTH if half == 0 else quarter * QUARTER + part * EIGHTH
            to = turn * QUARTER + part * EIGHTH
            for i in range(4):
                mixed[to:to + EIGHTH, i * rows:(i + 1) * rows] = factors[i][
                    pl.ds(pl.multiple_of(at, EIGHTH), EIGHTH), :
                ]
    factor = mixed[...]
    for at in range(0, TILE, 512):
        size = min(512, TILE - at)
        block = jnp.concatenate([b[:, pl.ds(pl.multiple_of(base + at, 128), size)] for b in blocks], axis=0)
        total = jnp.dot(factor, block, preferred_element_type=F32)
        here = slice(at, at + size)
        for turn in range(4):
            value = total[turn * QUARTER:(turn + 1) * QUARTER]
            if adds:
                value = value + extra[turn, :, here].astype(F32)
            held[turn, :, here] = value.astype(HALF)
            out = outs[turn] if adds else outs[0].at[turn]
            copies.append(
                pltpu.make_async_copy(held.at[turn, :, here], out.at[:, here], sems.at[len(copies)])
            )
            copies[-1].start()
    for copy in copies:
        copy.wait()


def cross(factors, blocks, tile, half, at, extra=None):
    rows, width = blocks[0].shape
    ranks = factors[0].shape[0]
    adds = extra is not None
    if adds:
        out_shape = [pltpu.HBM((QUARTER, TILE), HALF)] * 4
    else:
        out_shape = pltpu.HBM((4, QUARTER, TILE), HALF)
    return call(
        functools.partial(cross_kernel, half, adds),
        "cross_add" if adds else "cross",
        [jnp.stack([tile, at]).astype(jnp.int32), *factors, *blocks] + ([extra] if adds else []),
        out_shape,
        in_specs=[SMEM] + [VMEM] * (8 + adds),
        out_specs=[HBM] * 4 if adds else HBM,
        scratch=[
            pltpu.VMEM((ranks, 4 * rows), HALF),
            pltpu.VMEM((4, QUARTER, TILE), HALF),
            pltpu.SemaphoreType.DMA((16,)),
        ],
        flops=8 * rows * TILE * ranks,
    )


def fold_kernel(at_ref, *refs):
    terms, outs, (taken, held, in_sems, out_sems) = refs[:4], refs[4:8], refs[8:]
    loads = [pltpu.make_async_copy(terms[i], taken.at[i], in_sems.at[i]) for i in range(4)]
    stores = [pltpu.make_async_copy(held.at[i], outs[i], out_sems.at[i]) for i in range(4)]
    for load in loads:
        load.start()
    for load in loads:
        load.wait()
    for turn in range(4):
        at = lax.rem(at_ref[0] + turn, 4) * EIGHTH
        here = pl.ds(pl.multiple_of(at, EIGHTH), EIGHTH)
        total = taken[0, here, :].astype(F32)
        for i in range(1, 4):
            total += taken[i, here, :].astype(F32)
        held[turn] = total.astype(HALF)
        stores[turn].start()
    for store in stores:
        store.wait()


def fold(terms, at):
    return call(
        fold_kernel,
        "fold",
        [jnp.full((1,), at, jnp.int32), *in_hbm(terms)],
        [pltpu.HBM((EIGHTH, TILE), HALF)] * 4,
        in_specs=[SMEM] + [HBM] * 4,
        out_specs=[HBM] * 4,
        scratch=[
            pltpu.VMEM((4, QUARTER, TILE), HALF),
            pltpu.VMEM((4, EIGHTH, TILE), HALF),
            pltpu.SemaphoreType.DMA((4,)),
            pltpu.SemaphoreType.DMA((4,)),
        ],
        flops=4 * QUARTER * TILE,
    )


def finish_kernel(*refs):
    terms, out, (taken, held, in_sems, out_sem) = refs[:8], refs[8], refs[9:]
    loads = [pltpu.make_async_copy(terms[i], taken.at[i], in_sems.at[i]) for i in range(8)]
    for load in loads:
        load.start()
    for side in range(2):
        for load in loads[4 * side:4 * side + 4]:
            load.wait()
        total = taken[4 * side].astype(F32)
        for i in range(1, 4):
            total += taken[4 * side + i].astype(F32)
        held[side * EIGHTH:(side + 1) * EIGHTH, :] = total.astype(HALF)
    store = pltpu.make_async_copy(held, out, out_sem)
    store.start()
    store.wait()


def finish(first, second):
    return call(
        finish_kernel,
        "finish",
        in_hbm([*first, *second]),
        pltpu.HBM((2 * EIGHTH, TILE), HALF),
        in_specs=[HBM] * 8,
        out_specs=HBM,
        scratch=[
            pltpu.VMEM((8, EIGHTH, TILE), HALF),
            pltpu.VMEM((2 * EIGHTH, TILE), HALF),
            pltpu.SemaphoreType.DMA((8,)),
            pltpu.SemaphoreType.DMA,
        ],
        flops=8 * EIGHTH * TILE,
    )


def tile_of(total, tile):
    ranks = 16 * EIGHTH
    return total[:, tile % 2, tile // 2].reshape(ranks, TILE)


def right_kernel(rows_hbm, weights_hbm, total_hbm, raw_ref, squares_ref, weights_ref, total_ref, rows_ref, sems):
    count = raw_ref.shape[0]
    loads = [pltpu.make_async_copy(rows_hbm, rows_ref, sems.at[4])]
    for tile in range(4):
        here = (slice(None), tile % 2, tile // 2)
        loads.append(pltpu.make_async_copy(total_hbm.at[here], total_ref.at[here], sems.at[tile]))
    loads.append(pltpu.make_async_copy(weights_hbm, weights_ref, sems.at[5]))
    for load in loads:
        load.start()
    loads[0].wait()
    squares = 0.0
    for tile in range(4):
        loads[1 + tile].wait()
        both = jnp.dot(rows_ref[...], tile_of(total_ref, tile), preferred_element_type=F32)
        raw = both[:count] + both[count:]
        raw_ref[:, tile * TILE:(tile + 1) * TILE] = raw
        squares += jnp.sum(raw * raw, axis=1, keepdims=True)
    squares_ref[...] = jnp.broadcast_to(squares, squares_ref.shape)
    loads[5].wait()


def right_rows(rows, weights, total):
    count = rows.shape[0] // 2
    return call(
        right_kernel,
        "right_rows",
        in_hbm([rows, weights, total]),
        [
            jax.ShapeDtypeStruct((count, 4 * TILE), F32),
            jax.ShapeDtypeStruct((count, 128), F32),
            pltpu.VMEM(weights.shape, weights.dtype),
            pltpu.VMEM(total.shape, total.dtype),
        ],
        in_specs=[HBM] * 3,
        scratch=[pltpu.VMEM(rows.shape, rows.dtype), pltpu.SemaphoreType.DMA((6,))],
        flops=2 * rows.size * 4 * TILE,
    )


def feedback_kernel(at_ref, weights_ref, total_ref, *refs):
    blocks, out, (held, sems) = refs[:8], refs[8], refs[9:]
    rows = blocks[0].shape[0]
    ranks = 16 * EIGHTH
    copies = []
    for tile in range(4):
        for start in range(0, TILE, CHUNK):
            size = min(CHUNK, TILE - start)
            total = total_ref[:, tile % 2, tile // 2, :, start:start + size].reshape(ranks, size)
            here = (tile % 2) * TILE + start
            to = slice(tile * TILE + start, tile * TILE + start + size)
            for turn in range(4):
                part = jnp.dot(
                    weights_ref[turn * rows:(turn + 1) * rows, :], total, preferred_element_type=F32
                )
                at = lax.rem(at_ref[0] - turn + 4, 4) * rows
                held[pl.ds(pl.multiple_of(at, rows), rows), to] = (
                    blocks[4 * (tile // 2) + turn][:, here:here + size].astype(F32) - part
                ).astype(HALF)
            copies.append(pltpu.make_async_copy(held.at[:, to], out.at[:, to], sems.at[len(copies)]))
            copies[-1].start()
    for copy in copies:
        copy.wait()


def apply_feedback(weights, total, blocks, place):
    rows = blocks[0].shape[0]
    ranks = weights.shape[1]
    shape = (4 * rows, 4 * TILE)
    return call(
        feedback_kernel,
        "feedback",
        [jnp.full((1,), place, jnp.int32), weights, total, *blocks],
        pltpu.HBM(shape, HALF),
        in_specs=[SMEM] + [VMEM] * 10,
        out_specs=HBM,
        scratch=[pltpu.VMEM(shape, HALF), pltpu.SemaphoreType.DMA((4 * -(-TILE // CHUNK),))],
        flops=32 * rows * TILE * ranks,
    )


def after(value, *others):
    return lax.optimization_barrier((value,) + others)[0]


def per_device(momentum, gradient, right_factor):
    ranks_dev, width = right_factor.shape
    half_width = width // 2
    at_y, at_x, core, place = (lax.axis_index(name) for name in ("y", "x", "core", "col"))
    row = ("y", "x", "core")
    right_all = lax.all_gather(right_factor, row, axis=0, tiled=True)
    ranks = right_all.shape[0]
    blocks = [[None] * 4, [None] * 4]
    last = place
    for half in range(2):
        for turn in (2, 1, 3, 0):
            block = lax.rem(place + turn, 4) * 2 + half
            start = after(block, last) * half_width
            pair = [lax.dynamic_slice_in_dim(v, start, half_width, 1).astype(F32) for v in (momentum, gradient)]
            last = (pair[0] + pair[1]).astype(HALF)
            blocks[half][turn] = ring(last, "col", turn) if turn else last
    partial = project(blocks[0], right_all, 0)
    parts = project(blocks[1], right_all, 1, partial)
    terms = [parts[0]] + [ring(parts[turn], "col", -turn) for turn in (2, 1, 3)]
    mine, turned = settle(terms)
    factors = [turned] + [ring(turned, "col", turn) for turn in (1, 2, 3)]

    places = (at_x, at_y)
    sent = [cross(factors, blocks[half], 1 - core, half, places[half]) for half in range(2)]
    got = [swap_cores(value) for value in sent]
    first = list(cross(factors, blocks[0], after(core, sent[1]), 0, at_x, got[0]))
    second = list(cross(factors, blocks[1], after(core, first[0]), 1, at_y, got[1]))
    for turn in (2, 1, 3):
        first[turn] = ring(after(first[turn], second[0]), "x", turn)
        second[turn] = ring(second[turn], "y", turn)

    gram_part = gram_of([after(factors[0], first[2])] + factors[1:])
    rows = ranks // ranks_dev
    gram_pieces = lax.all_to_all(gram_part, row, split_axis=0, concat_axis=0, tiled=True)
    copies = spread(gram_pieces.reshape(rows, ranks_dev, ranks))

    first = list(fold(first, at_y))
    for turn in (2, 1, 3):
        first[turn] = ring(first[turn], "y", turn)
    second = list(fold(second, at_x))
    gram = lax.all_to_all(copies.reshape(ranks, ranks), row, split_axis=0, concat_axis=0, tiled=True)
    for turn in (2, 1, 3):
        second[turn] = ring(second[turn], "x", turn)
    done = finish([after(first[0], copies)] + first[1:], second)
    total = lax.all_gather(done, row, axis=0, tiled=True)
    total = total.reshape(16, 2, 2, EIGHTH, TILE)

    at_row = (at_y * 4 + at_x) * 2 + core
    own, weights, left_factor = factorize(after(gram, done), factors, at_row, ranks_dev)

    right_raw, squares, weights, total = right_rows(own, weights, total)
    squares = squares + sum(ring(squares, "col", turn) for turn in (1, 2, 3))
    new_momentum = apply_feedback(weights, total, blocks[0] + blocks[1], place)
    new_right = right_raw / jnp.sqrt(squares[:, :1] + 1e-06)
    return (new_momentum, left_factor, new_right)


def solution(mesh):
    fine = Mesh(mesh.devices.reshape(4, 4, 2, 4), ("y", "x", "core", "col"))
    every = ("y", "x", "core", "col")
    row = ("y", "x", "core")
    in_specs = (P(every, None), P(every, None), P(row, "col"))
    out_specs = (P(row, "col"), P(every, None), P(row, "col"))
    return jax.shard_map(
        per_device, mesh=fine, in_specs=in_specs, out_specs=out_specs, check_vma=False
    )
```

```python
import functools
import math

import jax
import jax.numpy as jnp
from jax import lax
from jax.experimental import pallas as pl
from jax.experimental.pallas import tpu as pltpu
from jax.sharding import Mesh, PartitionSpec as P

D = 16384
HI=lax.Precision.HIGHEST
B=128
PANEL=8

def total(terms):
    while len(terms) > 1:
        terms = [sum(terms[i:i + 2][1:], terms[i]) for i in range(0, len(terms), 2)]
    return terms[0]


def diagonal_inverse(a_ref, x_ref):
    row = lax.broadcasted_iota(jnp.int32, (B, B), 0)
    col = lax.broadcasted_iota(jnp.int32, (B, B), 1)
    x_ref[...] = jnp.where(row == col, 1.0, 0.0)
    panels = B // PANEL
    full = (PANEL, B)
    for p in range(panels):
        at = p * PANEL
        mine = a_ref[at:at + PANEL, :]
        xmine = x_ref[at:at + PANEL, :]
        cols = [jnp.broadcast_to(mine[:, at + j:at + j + 1], full) for j in range(PANEL)]
        a = {(i, j): jnp.broadcast_to(cols[j][i:i + 1, :], full) for j in range(PANEL) for i in range(j, PANEL)}
        low = {}
        for k in range(PANEL):
            root = lax.rsqrt(a[k, k])
            for i in range(k + 1, PANEL):
                a[i, k] = a[i, k] * root
            for j in range(k + 1, PANEL):
                for i in range(j, PANEL):
                    a[i, j] = a[i, j] - a[i, k] * a[j, k]
            for j in range(k):
                low[k, j] = -root * total([a[k, i] * low[i, j] for i in range(j, k)])
            low[k, k] = root

        def forward(block):
            r = [jnp.broadcast_to(block[i:i + 1, :], full) for i in range(PANEL)]
            return [total([low[i, j] * r[j] for j in range(i + 1)]) for i in range(PANEL)]

        def backward(y):
            return [total([low[j, i] * y[j] for j in range(i, PANEL)]) for i in range(PANEL)]

        yx = forward(xmine)
        sub = lax.broadcasted_iota(jnp.int32, full, 0)
        out = yx[0]
        for i in range(1, PANEL):
            out = jnp.where(sub == i, yx[i], out)
        x_ref[at:at + PANEL, :] = out
        if p + 1 < panels:
            za = backward(forward(mine))
            zx = backward(yx)
            for q in range(p + 1, panels):
                s = slice(q * PANEL, (q + 1) * PANEL)
                block = a_ref[s, :]
                m = [jnp.broadcast_to(block[:, at + j:at + j + 1], full) for j in range(PANEL)]
                a_ref[s, :] = block - total([m[j] * za[j] for j in range(PANEL)])
                x_ref[s, :] = x_ref[s, :] - total([m[j] * zx[j] for j in range(PANEL)])

def factor_kernel(at_ref, g_ref, *refs):
    factors, outs, scratch = refs[:4], refs[4:7], refs[7:]
    own_ref, weights_ref, left_ref, a_s, x_ref, d_s, i_s, sems = scratch
    copies = [
        pltpu.make_async_copy(ref, out, sems.at[i])
        for i, (ref, out) in enumerate(zip((own_ref, weights_ref, left_ref), outs))
    ]
    n = g_ref.shape[0]
    nb = n // B
    a_s[...] = g_ref[...].astype(jnp.float32)
    x_ref[...] = jnp.zeros_like(x_ref)

    def split(value):
        high = value.astype(jnp.bfloat16)
        return high, (value - high.astype(jnp.float32)).astype(jnp.bfloat16)

    def half_dot(u, v, dims):
        return lax.dot_general(u, v, (dims, ((), ())), preferred_element_type=jnp.float32)

    def dot(u, v, dims):
        (u_high, u_low), (v_high, v_low) = u, v
        return half_dot(u_high, v_high, dims) + (half_dot(u_high, v_low, dims) + half_dot(u_low, v_high, dims))

    def step(b, _):
        at = pl.multiple_of(b * B, B)
        here = pl.ds(at, B)
        d_s[...] = a_s[here, here]
        diagonal_inverse(d_s, i_s)
        for k in range(nb):
            @pl.when(b == k)
            def _(here=slice(k * B, (k + 1) * B), before=k * B, rest=slice((k + 1) * B, n)):
                inv = split(i_s[...])
                x_ref[here, here] = i_s[...]
                if before:
                    x_ref[here, :before] = dot(inv, split(x_ref[here, :before]), ((1,), (0,)))
                if rest.start < n:
                    y_x = split(x_ref[here, :here.stop])
                    y_a = split(dot(inv, split(a_s[here, rest]), ((1,), (0,))))
                    a_s[rest, rest] = a_s[rest, rest] - dot(y_a, y_a, ((0,), (0,)))
                    x_ref[rest, :here.stop] = x_ref[rest, :here.stop] - dot(y_a, y_x, ((0,), (0,)))
        return 0

    lax.fori_loop(0, nb, step, 0)

    count = own_ref.shape[0] // 2
    own = x_ref[pl.ds(pl.multiple_of(at_ref[0] * count, count), count), :]
    own_ref[:count, :], own_ref[count:, :] = split(own)
    copies[0].start()
    high, low = split(x_ref[...])
    factor = jnp.concatenate([f[...] for f in factors], axis=1)
    turned = half_dot(high, factor, ((1,), (0,))) + half_dot(low, factor, ((1,), (0,)))
    rows = left_ref.shape[0]
    left_ref[...] = turned[:, :rows].T * float(D) ** 0.5
    copies[2].start()
    turned_high, turned_low = split(turned)
    weights = half_dot(turned_high, high, ((0,), (0,)))
    weights += half_dot(turned_low, high, ((0,), (0,)))
    weights += half_dot(turned_high, low, ((0,), (0,)))
    weights_ref[...] = (0.75 * weights).astype(jnp.bfloat16)
    copies[1].start()
    for copy in copies:
        copy.wait()


def factorize(gram, factors, place, count):
    n = gram.shape[0]
    rows = factors[0].shape[1]
    vmem = pl.BlockSpec(memory_space=pltpu.VMEM)
    outs = [((2 * count, n), jnp.bfloat16), ((4 * rows, n), jnp.bfloat16), ((rows, n), jnp.float32)]
    return pl.pallas_call(
        factor_kernel,
        out_shape=[pltpu.HBM(*out) for out in outs],
        in_specs=[pl.BlockSpec(memory_space=pltpu.SMEM)] + [vmem] * 5,
        out_specs=[pl.BlockSpec(memory_space=pltpu.HBM)] * 3,
        scratch_shapes=[pltpu.VMEM(*out) for out in outs]
        + [pltpu.VMEM((n, n), jnp.float32)] * 2
        + [pltpu.VMEM((B, B), jnp.float32)] * 2
        + [pltpu.SemaphoreType.DMA((3,))],
        compiler_params=pltpu.CompilerParams(vmem_limit_bytes=16 * 2**20),
        cost_estimate=pl.CostEstimate(flops=2 * 10**10, bytes_accessed=4 * 2**20, transcendentals=0),
        name="factorize",
    )(jnp.full((1,), place, jnp.int32), gram, *factors)


TILE = 1664
CHUNK = 512
QUARTER = 128
EIGHTH = 32
F32 = jnp.float32
HALF = jnp.bfloat16
VMEM = pl.BlockSpec(memory_space=pltpu.VMEM)
SMEM = pl.BlockSpec(memory_space=pltpu.SMEM)
HBM = pl.BlockSpec(memory_space=pltpu.HBM)


def ring(value, axis, shift):
    size = lax.axis_size(axis)
    return lax.ppermute(value, axis, [(i, (i + shift) % size) for i in range(size)])


def swap_cores(value):
    return lax.ppermute(value, "core", [(0, 1), (1, 0)])


def in_hbm(values):
    return [pltpu.with_memory_space_constraint(value, pltpu.HBM) for value in values]


def call(kernel, name, operands, out_shape, scratch=(), in_specs=None, out_specs=None, flops=0, moved=None):
    shapes = out_shape if isinstance(out_shape, list) else [out_shape]
    if moved is None:
        moved = sum(math.prod(v.shape) * v.dtype.itemsize for v in list(operands) + shapes)
    return pl.pallas_call(
        kernel,
        in_specs=in_specs or [VMEM] * len(operands),
        out_specs=out_specs or ([VMEM] * len(shapes) if isinstance(out_shape, list) else VMEM),
        out_shape=out_shape,
        scratch_shapes=list(scratch),
        compiler_params=pltpu.CompilerParams(vmem_limit_bytes=16 * 2**20),
        cost_estimate=pl.CostEstimate(flops=int(flops), bytes_accessed=int(moved), transcendentals=0),
        name=name,
    )(*operands)


def blend_kernel(at_ref, momentum, gradient, out, held, sems):
    width = out.shape[1]
    loads = []
    for start in range(0, width, TILE):
        here = pl.ds(pl.multiple_of(at_ref[0] * width + start, 128), TILE)
        for i, source in enumerate((momentum, gradient)):
            target = held.at[i, :, start:start + TILE]
            loads.append(pltpu.make_async_copy(source.at[:, here], target, sems.at[len(loads)]))
            loads[-1].start()
    for start in range(0, width, TILE):
        for load in loads[2 * start // TILE:2 * start // TILE + 2]:
            load.wait()
        here = slice(start, start + TILE)
        out[:, here] = (held[0, :, here].astype(F32) + held[1, :, here].astype(F32)).astype(HALF)


def blend_block(momentum, gradient, block, width):
    rows = momentum.shape[0]
    return call(
        blend_kernel,
        "blend",
        [jnp.full((1,), block, jnp.int32), *in_hbm([momentum, gradient])],
        jax.ShapeDtypeStruct((rows, width), HALF),
        in_specs=[SMEM, HBM, HBM],
        scratch=[pltpu.VMEM((2, rows, width), HALF), pltpu.SemaphoreType.DMA((2 * width // TILE,))],
        flops=rows * width,
        moved=rows * width,
    )


def project_kernel(half, *refs):
    blocks, right = refs[:4], refs[4]
    rows, width = blocks[0].shape
    total = refs[5][...] if half else 0.0
    for at in range(0, width, TILE):
        block = jnp.concatenate([b[:, at:at + TILE] for b in blocks], axis=0)
        total += lax.dot_general(
            block,
            right[:, half * width + at:half * width + at + TILE],
            (((1,), (1,)), ((), ())),
            preferred_element_type=F32,
        )
    if half:
        for i, out in enumerate(refs[6:]):
            out[...] = total[i * rows:(i + 1) * rows].astype(HALF)
    else:
        refs[5][...] = total


def project(blocks, right, half, before=None):
    rows, width = blocks[0].shape
    ranks = right.shape[0]
    if half:
        out_shape = [jax.ShapeDtypeStruct((rows, ranks), HALF)] * 4
    else:
        out_shape = jax.ShapeDtypeStruct((4 * rows, ranks), F32)
    return call(
        functools.partial(project_kernel, half),
        "project",
        [*blocks, right] + ([before] if half else []),
        out_shape,
        flops=8 * rows * width * ranks,
    )


def settle_kernel(*refs):
    terms, out, turned = refs[:4], refs[4], refs[5]
    total = terms[0][...].astype(F32)
    for term in terms[1:]:
        total += term[...].astype(F32)
    out[...] = total.astype(HALF)
    turned[...] = total.T.astype(HALF)


def settle(terms):
    rows, ranks = terms[0].shape
    return call(
        settle_kernel,
        "settle",
        terms,
        [jax.ShapeDtypeStruct((rows, ranks), HALF), jax.ShapeDtypeStruct((ranks, rows), HALF)],
        flops=4 * rows * ranks,
    )


def gram_kernel(*refs):
    total = 0.0
    for factor in refs[:4]:
        total += lax.dot_general(
            factor[...], factor[...], (((1,), (1,)), ((), ())), preferred_element_type=F32
        )
    refs[4][...] = total.astype(HALF)


def gram_of(factors):
    ranks, rows = factors[0].shape
    return call(
        gram_kernel,
        "gram",
        factors,
        jax.ShapeDtypeStruct((ranks, ranks), HALF),
        flops=8 * rows * ranks * ranks,
    )


def spread_kernel(pieces_ref, out_ref):
    total = pieces_ref[0].astype(F32)
    for i in range(1, pieces_ref.shape[0]):
        total += pieces_ref[i].astype(F32)
    out_ref[...] = jnp.broadcast_to(total.astype(HALF)[None], out_ref.shape)


def spread(pieces):
    return call(spread_kernel, "spread", [pieces], jax.ShapeDtypeStruct(pieces.shape, HALF), flops=pieces.size)


def cross_kernel(half, adds, at_ref, *refs):
    factors, blocks = refs[:4], refs[4:8]
    extra = refs[8] if adds else None
    outs, (mixed, held, sems) = refs[8 + adds:-3], refs[-3:]
    rows = blocks[0].shape[0]
    base = pl.multiple_of(at_ref[0] * TILE, 128)
    copies = []
    for turn in range(4):
        quarter = lax.rem(at_ref[1] + turn, 4)
        for part in range(4):
            at = part * QUARTER + quarter * EIGHTH if half == 0 else quarter * QUARTER + part * EIGHTH
            to = turn * QUARTER + part * EIGHTH
            for i in range(4):
                mixed[to:to + EIGHTH, i * rows:(i + 1) * rows] = factors[i][
                    pl.ds(pl.multiple_of(at, EIGHTH), EIGHTH), :
                ]
    factor = mixed[...]
    for at in range(0, TILE, 512):
        size = min(512, TILE - at)
        block = jnp.concatenate([b[:, pl.ds(pl.multiple_of(base + at, 128), size)] for b in blocks], axis=0)
        total = jnp.dot(factor, block, preferred_element_type=F32)
        here = slice(at, at + size)
        for turn in range(4):
            value = total[turn * QUARTER:(turn + 1) * QUARTER]
            if adds:
                value = value + extra[turn, :, here].astype(F32)
            held[turn, :, here] = value.astype(HALF)
            out = outs[turn] if adds else outs[0].at[turn]
            copies.append(
                pltpu.make_async_copy(held.at[turn, :, here], out.at[:, here], sems.at[len(copies)])
            )
            copies[-1].start()
    for copy in copies:
        copy.wait()


def cross(factors, blocks, tile, half, at, extra=None):
    rows, width = blocks[0].shape
    ranks = factors[0].shape[0]
    adds = extra is not None
    if adds:
        out_shape = [pltpu.HBM((QUARTER, TILE), HALF)] * 4
    else:
        out_shape = pltpu.HBM((4, QUARTER, TILE), HALF)
    return call(
        functools.partial(cross_kernel, half, adds),
        "cross_add" if adds else "cross",
        [jnp.stack([tile, at]).astype(jnp.int32), *factors, *blocks] + ([extra] if adds else []),
        out_shape,
        in_specs=[SMEM] + [VMEM] * (8 + adds),
        out_specs=[HBM] * 4 if adds else HBM,
        scratch=[
            pltpu.VMEM((ranks, 4 * rows), HALF),
            pltpu.VMEM((4, QUARTER, TILE), HALF),
            pltpu.SemaphoreType.DMA((16,)),
        ],
        flops=8 * rows * TILE * ranks,
    )


def fold_kernel(at_ref, *refs):
    terms, outs, (taken, held, in_sems, out_sems) = refs[:4], refs[4:8], refs[8:]
    loads = [pltpu.make_async_copy(terms[i], taken.at[i], in_sems.at[i]) for i in range(4)]
    stores = [pltpu.make_async_copy(held.at[i], outs[i], out_sems.at[i]) for i in range(4)]
    for load in loads:
        load.start()
    for load in loads:
        load.wait()
    for turn in range(4):
        at = lax.rem(at_ref[0] + turn, 4) * EIGHTH
        here = pl.ds(pl.multiple_of(at, EIGHTH), EIGHTH)
        total = taken[0, here, :].astype(F32)
        for i in range(1, 4):
            total += taken[i, here, :].astype(F32)
        held[turn] = total.astype(HALF)
        stores[turn].start()
    for store in stores:
        store.wait()


def fold(terms, at):
    return call(
        fold_kernel,
        "fold",
        [jnp.full((1,), at, jnp.int32), *in_hbm(terms)],
        [pltpu.HBM((EIGHTH, TILE), HALF)] * 4,
        in_specs=[SMEM] + [HBM] * 4,
        out_specs=[HBM] * 4,
        scratch=[
            pltpu.VMEM((4, QUARTER, TILE), HALF),
            pltpu.VMEM((4, EIGHTH, TILE), HALF),
            pltpu.SemaphoreType.DMA((4,)),
            pltpu.SemaphoreType.DMA((4,)),
        ],
        flops=4 * QUARTER * TILE,
    )


def finish_kernel(*refs):
    terms, out, (taken, held, in_sems, out_sem) = refs[:8], refs[8], refs[9:]
    loads = [pltpu.make_async_copy(terms[i], taken.at[i], in_sems.at[i]) for i in range(8)]
    for load in loads:
        load.start()
    for side in range(2):
        for load in loads[4 * side:4 * side + 4]:
            load.wait()
        total = taken[4 * side].astype(F32)
        for i in range(1, 4):
            total += taken[4 * side + i].astype(F32)
        held[side * EIGHTH:(side + 1) * EIGHTH, :] = total.astype(HALF)
    store = pltpu.make_async_copy(held, out, out_sem)
    store.start()
    store.wait()


def finish(first, second):
    return call(
        finish_kernel,
        "finish",
        in_hbm([*first, *second]),
        pltpu.HBM((2 * EIGHTH, TILE), HALF),
        in_specs=[HBM] * 8,
        out_specs=HBM,
        scratch=[
            pltpu.VMEM((8, EIGHTH, TILE), HALF),
            pltpu.VMEM((2 * EIGHTH, TILE), HALF),
            pltpu.SemaphoreType.DMA((8,)),
            pltpu.SemaphoreType.DMA,
        ],
        flops=8 * EIGHTH * TILE,
    )


def tile_of(total, tile):
    ranks = 16 * EIGHTH
    return total[:, tile % 2, tile // 2].reshape(ranks, TILE)


def right_kernel(rows_hbm, weights_hbm, total_hbm, raw_ref, squares_ref, weights_ref, total_ref, rows_ref, sems):
    count = raw_ref.shape[0]
    loads = [pltpu.make_async_copy(rows_hbm, rows_ref, sems.at[4])]
    for tile in range(4):
        here = (slice(None), tile % 2, tile // 2)
        loads.append(pltpu.make_async_copy(total_hbm.at[here], total_ref.at[here], sems.at[tile]))
    loads.append(pltpu.make_async_copy(weights_hbm, weights_ref, sems.at[5]))
    for load in loads:
        load.start()
    loads[0].wait()
    squares = 0.0
    for tile in range(4):
        loads[1 + tile].wait()
        both = jnp.dot(rows_ref[...], tile_of(total_ref, tile), preferred_element_type=F32)
        raw = both[:count] + both[count:]
        raw_ref[:, tile * TILE:(tile + 1) * TILE] = raw
        squares += jnp.sum(raw * raw, axis=1, keepdims=True)
    squares_ref[...] = jnp.broadcast_to(squares, squares_ref.shape)
    loads[5].wait()


def right_rows(rows, weights, total):
    count = rows.shape[0] // 2
    return call(
        right_kernel,
        "right_rows",
        in_hbm([rows, weights, total]),
        [
            jax.ShapeDtypeStruct((count, 4 * TILE), F32),
            jax.ShapeDtypeStruct((count, 128), F32),
            pltpu.VMEM(weights.shape, weights.dtype),
            pltpu.VMEM(total.shape, total.dtype),
        ],
        in_specs=[HBM] * 3,
        scratch=[pltpu.VMEM(rows.shape, rows.dtype), pltpu.SemaphoreType.DMA((6,))],
        flops=2 * rows.size * 4 * TILE,
    )


def feedback_kernel(at_ref, weights_ref, total_ref, *refs):
    blocks, out, (held, sems) = refs[:8], refs[8], refs[9:]
    rows = blocks[0].shape[0]
    ranks = 16 * EIGHTH
    copies = []
    for tile in range(4):
        for start in range(0, TILE, CHUNK):
            size = min(CHUNK, TILE - start)
            total = total_ref[:, tile % 2, tile // 2, :, start:start + size].reshape(ranks, size)
            here = (tile % 2) * TILE + start
            to = slice(tile * TILE + start, tile * TILE + start + size)
            for turn in range(4):
                part = jnp.dot(
                    weights_ref[turn * rows:(turn + 1) * rows, :], total, preferred_element_type=F32
                )
                at = lax.rem(at_ref[0] - turn + 4, 4) * rows
                held[pl.ds(pl.multiple_of(at, rows), rows), to] = (
                    blocks[4 * (tile // 2) + turn][:, here:here + size].astype(F32) - part
                ).astype(HALF)
            copies.append(pltpu.make_async_copy(held.at[:, to], out.at[:, to], sems.at[len(copies)]))
            copies[-1].start()
    for copy in copies:
        copy.wait()


def apply_feedback(weights, total, blocks, place):
    rows = blocks[0].shape[0]
    ranks = weights.shape[1]
    shape = (4 * rows, 4 * TILE)
    return call(
        feedback_kernel,
        "feedback",
        [jnp.full((1,), place, jnp.int32), weights, total, *blocks],
        pltpu.HBM(shape, HALF),
        in_specs=[SMEM] + [VMEM] * 10,
        out_specs=HBM,
        scratch=[pltpu.VMEM(shape, HALF), pltpu.SemaphoreType.DMA((4 * -(-TILE // CHUNK),))],
        flops=32 * rows * TILE * ranks,
    )


def after(value, *others):
    return lax.optimization_barrier((value,) + others)[0]


def per_device(momentum, gradient, right_factor):
    ranks_dev, width = right_factor.shape
    half_width = width // 2
    at_y, at_x, core, place = (lax.axis_index(name) for name in ("y", "x", "core", "col"))
    row = ("y", "x", "core")
    right_all = lax.all_gather(right_factor, row, axis=0, tiled=True)
    ranks = right_all.shape[0]
    blocks = [[None] * 4, [None] * 4]
    for half in range(2):
        for turn in (2, 1, 3, 0):
            block = lax.rem(place + turn, 4) * 2 + half
            mine = blend_block(momentum, gradient, after(block, blocks[0][0]) if half else block, half_width)
            blocks[half][turn] = ring(mine, "col", turn) if turn else mine
    partial = project(blocks[0], right_all, 0)
    parts = project(blocks[1], right_all, 1, partial)
    terms = [parts[0]] + [ring(parts[turn], "col", -turn) for turn in (2, 1, 3)]
    mine, turned = settle(terms)
    factors = [turned] + [ring(turned, "col", turn) for turn in (1, 2, 3)]

    places = (at_x, at_y)
    sent = [cross(factors, blocks[half], 1 - core, half, places[half]) for half in range(2)]
    got = [swap_cores(value) for value in sent]
    first = list(cross(factors, blocks[0], after(core, sent[1]), 0, at_x, got[0]))
    second = list(cross(factors, blocks[1], after(core, first[0]), 1, at_y, got[1]))
    for turn in (2, 1, 3):
        first[turn] = ring(after(first[turn], second[0]), "x", turn)
        second[turn] = ring(second[turn], "y", turn)

    gram_part = gram_of([after(factors[0], first[1])] + factors[1:])
    rows = ranks // ranks_dev
    gram_pieces = lax.all_to_all(gram_part, row, split_axis=0, concat_axis=0, tiled=True)

    first = list(fold(first, at_y))
    for turn in (2, 1, 3):
        first[turn] = ring(first[turn], "y", turn)
    second = list(fold(second, at_x))
    for turn in (2, 1, 3):
        second[turn] = ring(second[turn], "x", turn)
    first[0], gram_pieces = lax.optimization_barrier((first[0], gram_pieces))
    done = finish(first, second)
    copies = spread(gram_pieces.reshape(rows, ranks_dev, ranks))
    gram = lax.all_to_all(copies.reshape(ranks, ranks), row, split_axis=0, concat_axis=0, tiled=True)
    total = lax.all_gather(done, row, axis=0, tiled=True)
    total = total.reshape(16, 2, 2, EIGHTH, TILE)

    at_row = (at_y * 4 + at_x) * 2 + core
    own, weights, left_factor = factorize(after(gram, done), factors, at_row, ranks_dev)

    right_raw, squares, weights, total = right_rows(own, weights, total)
    squares = squares + sum(ring(squares, "col", turn) for turn in (1, 2, 3))
    new_momentum = apply_feedback(weights, total, blocks[0] + blocks[1], place)
    new_right = right_raw / jnp.sqrt(squares[:, :1] + 1e-06)
    return (new_momentum, left_factor, new_right)


def solution(mesh):
    fine = Mesh(mesh.devices.reshape(4, 4, 2, 4), ("y", "x", "core", "col"))
    every = ("y", "x", "core", "col")
    row = ("y", "x", "core")
    in_specs = (P(every, None), P(every, None), P(row, "col"))
    out_specs = (P(row, "col"), P(every, None), P(row, "col"))
    return jax.shard_map(
        per_device, mesh=fine, in_specs=in_specs, out_specs=out_specs, check_vma=False
    )
```

```python
import functools
import math

import jax
import jax.numpy as jnp
from jax import lax
from jax.experimental import pallas as pl
from jax.experimental.pallas import tpu as pltpu
from jax.sharding import Mesh, PartitionSpec as P

D = 16384
HI=lax.Precision.HIGHEST
B=128
PANEL=8

def total(terms):
    while len(terms) > 1:
        terms = [sum(terms[i:i + 2][1:], terms[i]) for i in range(0, len(terms), 2)]
    return terms[0]


def diagonal_inverse(a_ref, x_ref):
    row = lax.broadcasted_iota(jnp.int32, (B, B), 0)
    col = lax.broadcasted_iota(jnp.int32, (B, B), 1)
    x_ref[...] = jnp.where(row == col, 1.0, 0.0)
    panels = B // PANEL
    full = (PANEL, B)
    for p in range(panels):
        at = p * PANEL
        mine = a_ref[at:at + PANEL, :]
        xmine = x_ref[at:at + PANEL, :]
        cols = [jnp.broadcast_to(mine[:, at + j:at + j + 1], full) for j in range(PANEL)]
        a = {(i, j): jnp.broadcast_to(cols[j][i:i + 1, :], full) for j in range(PANEL) for i in range(j, PANEL)}
        low = {}
        for k in range(PANEL):
            root = lax.rsqrt(a[k, k])
            for i in range(k + 1, PANEL):
                a[i, k] = a[i, k] * root
            for j in range(k + 1, PANEL):
                for i in range(j, PANEL):
                    a[i, j] = a[i, j] - a[i, k] * a[j, k]
            for j in range(k):
                low[k, j] = -root * total([a[k, i] * low[i, j] for i in range(j, k)])
            low[k, k] = root

        def forward(block):
            r = [jnp.broadcast_to(block[i:i + 1, :], full) for i in range(PANEL)]
            return [total([low[i, j] * r[j] for j in range(i + 1)]) for i in range(PANEL)]

        def backward(y):
            return [total([low[j, i] * y[j] for j in range(i, PANEL)]) for i in range(PANEL)]

        yx = forward(xmine)
        sub = lax.broadcasted_iota(jnp.int32, full, 0)
        out = yx[0]
        for i in range(1, PANEL):
            out = jnp.where(sub == i, yx[i], out)
        x_ref[at:at + PANEL, :] = out
        if p + 1 < panels:
            za = backward(forward(mine))
            zx = backward(yx)
            for q in range(p + 1, panels):
                s = slice(q * PANEL, (q + 1) * PANEL)
                block = a_ref[s, :]
                m = [jnp.broadcast_to(block[:, at + j:at + j + 1], full) for j in range(PANEL)]
                a_ref[s, :] = block - total([m[j] * za[j] for j in range(PANEL)])
                x_ref[s, :] = x_ref[s, :] - total([m[j] * zx[j] for j in range(PANEL)])

def factor_kernel(at_ref, g_ref, *refs):
    factors, outs, scratch = refs[:4], refs[4:7], refs[7:]
    own_ref, weights_ref, left_ref, a_s, x_ref, d_s, i_s, sems = scratch
    copies = [
        pltpu.make_async_copy(ref, out, sems.at[i])
        for i, (ref, out) in enumerate(zip((own_ref, weights_ref, left_ref), outs))
    ]
    n = g_ref.shape[0]
    nb = n // B
    a_s[...] = g_ref[...].astype(jnp.float32)
    x_ref[...] = jnp.zeros_like(x_ref)

    def split(value):
        high = value.astype(jnp.bfloat16)
        return high, (value - high.astype(jnp.float32)).astype(jnp.bfloat16)

    def half_dot(u, v, dims):
        return lax.dot_general(u, v, (dims, ((), ())), preferred_element_type=jnp.float32)

    def dot(u, v, dims):
        (u_high, u_low), (v_high, v_low) = u, v
        return half_dot(u_high, v_high, dims) + (half_dot(u_high, v_low, dims) + half_dot(u_low, v_high, dims))

    def step(b, _):
        at = pl.multiple_of(b * B, B)
        here = pl.ds(at, B)
        d_s[...] = a_s[here, here]
        diagonal_inverse(d_s, i_s)
        for k in range(nb):
            @pl.when(b == k)
            def _(here=slice(k * B, (k + 1) * B), before=k * B, rest=slice((k + 1) * B, n)):
                inv = split(i_s[...])
                x_ref[here, here] = i_s[...]
                if before:
                    x_ref[here, :before] = dot(inv, split(x_ref[here, :before]), ((1,), (0,)))
                if rest.start < n:
                    y_x = split(x_ref[here, :here.stop])
                    y_a = split(dot(inv, split(a_s[here, rest]), ((1,), (0,))))
                    a_s[rest, rest] = a_s[rest, rest] - dot(y_a, y_a, ((0,), (0,)))
                    x_ref[rest, :here.stop] = x_ref[rest, :here.stop] - dot(y_a, y_x, ((0,), (0,)))
        return 0

    lax.fori_loop(0, nb, step, 0)

    count = own_ref.shape[0] // 2
    own = x_ref[pl.ds(pl.multiple_of(at_ref[0] * count, count), count), :]
    own_ref[:count, :], own_ref[count:, :] = split(own)
    copies[0].start()
    high, low = split(x_ref[...])
    factor = jnp.concatenate([f[...] for f in factors], axis=1)
    turned = half_dot(high, factor, ((1,), (0,))) + half_dot(low, factor, ((1,), (0,)))
    rows = left_ref.shape[0]
    left_ref[...] = turned[:, :rows].T * float(D) ** 0.5
    copies[2].start()
    turned_high, turned_low = split(turned)
    weights = half_dot(turned_high, high, ((0,), (0,)))
    weights += half_dot(turned_low, high, ((0,), (0,)))
    weights += half_dot(turned_high, low, ((0,), (0,)))
    weights_ref[...] = (0.75 * weights).astype(jnp.bfloat16)
    copies[1].start()
    for copy in copies:
        copy.wait()


def factorize(gram, factors, place, count):
    n = gram.shape[0]
    rows = factors[0].shape[1]
    vmem = pl.BlockSpec(memory_space=pltpu.VMEM)
    outs = [((2 * count, n), jnp.bfloat16), ((4 * rows, n), jnp.bfloat16), ((rows, n), jnp.float32)]
    return pl.pallas_call(
        factor_kernel,
        out_shape=[pltpu.HBM(*out) for out in outs],
        in_specs=[pl.BlockSpec(memory_space=pltpu.SMEM)] + [vmem] * 5,
        out_specs=[pl.BlockSpec(memory_space=pltpu.HBM)] * 3,
        scratch_shapes=[pltpu.VMEM(*out) for out in outs]
        + [pltpu.VMEM((n, n), jnp.float32)] * 2
        + [pltpu.VMEM((B, B), jnp.float32)] * 2
        + [pltpu.SemaphoreType.DMA((3,))],
        compiler_params=pltpu.CompilerParams(vmem_limit_bytes=16 * 2**20),
        cost_estimate=pl.CostEstimate(flops=2 * 10**10, bytes_accessed=4 * 2**20, transcendentals=0),
        name="factorize",
    )(jnp.full((1,), place, jnp.int32), gram, *factors)


TILE = 1664
CHUNK = 512
QUARTER = 128
EIGHTH = 32
F32 = jnp.float32
HALF = jnp.bfloat16
VMEM = pl.BlockSpec(memory_space=pltpu.VMEM)
SMEM = pl.BlockSpec(memory_space=pltpu.SMEM)
HBM = pl.BlockSpec(memory_space=pltpu.HBM)


def ring(value, axis, shift):
    size = lax.axis_size(axis)
    return lax.ppermute(value, axis, [(i, (i + shift) % size) for i in range(size)])


def swap_cores(value):
    return lax.ppermute(value, "core", [(0, 1), (1, 0)])


def in_hbm(values):
    return [pltpu.with_memory_space_constraint(value, pltpu.HBM) for value in values]


def call(kernel, name, operands, out_shape, scratch=(), in_specs=None, out_specs=None, flops=0):
    shapes = out_shape if isinstance(out_shape, list) else [out_shape]
    moved = sum(math.prod(v.shape) * v.dtype.itemsize for v in list(operands) + shapes)
    return pl.pallas_call(
        kernel,
        in_specs=in_specs or [VMEM] * len(operands),
        out_specs=out_specs or ([VMEM] * len(shapes) if isinstance(out_shape, list) else VMEM),
        out_shape=out_shape,
        scratch_shapes=list(scratch),
        compiler_params=pltpu.CompilerParams(vmem_limit_bytes=16 * 2**20),
        cost_estimate=pl.CostEstimate(flops=int(flops), bytes_accessed=int(moved), transcendentals=0),
        name=name,
    )(*operands)


def project_kernel(half, *refs):
    blocks, right = refs[:4], refs[4]
    rows, width = blocks[0].shape
    total = refs[5][...] if half else 0.0
    for at in range(0, width, TILE):
        block = jnp.concatenate([b[:, at:at + TILE] for b in blocks], axis=0)
        total += lax.dot_general(
            block,
            right[:, half * width + at:half * width + at + TILE],
            (((1,), (1,)), ((), ())),
            preferred_element_type=F32,
        )
    if half:
        for i, out in enumerate(refs[6:]):
            out[...] = total[i * rows:(i + 1) * rows].astype(HALF)
    else:
        refs[5][...] = total


def project(blocks, right, half, before=None):
    rows, width = blocks[0].shape
    ranks = right.shape[0]
    if half:
        out_shape = [jax.ShapeDtypeStruct((rows, ranks), HALF)] * 4
    else:
        out_shape = jax.ShapeDtypeStruct((4 * rows, ranks), F32)
    return call(
        functools.partial(project_kernel, half),
        "project",
        [*blocks, right] + ([before] if half else []),
        out_shape,
        flops=8 * rows * width * ranks,
    )


def settle_kernel(*refs):
    terms, out, turned = refs[:4], refs[4], refs[5]
    total = terms[0][...].astype(F32)
    for term in terms[1:]:
        total += term[...].astype(F32)
    out[...] = total.astype(HALF)
    turned[...] = total.T.astype(HALF)


def settle(terms):
    rows, ranks = terms[0].shape
    return call(
        settle_kernel,
        "settle",
        terms,
        [jax.ShapeDtypeStruct((rows, ranks), HALF), jax.ShapeDtypeStruct((ranks, rows), HALF)],
        flops=4 * rows * ranks,
    )


def gram_kernel(*refs):
    total = 0.0
    for factor in refs[:4]:
        total += lax.dot_general(
            factor[...], factor[...], (((1,), (1,)), ((), ())), preferred_element_type=F32
        )
    out, held, sem = refs[4:]
    held[...] = total.astype(HALF)
    store = pltpu.make_async_copy(held, out, sem)
    store.start()
    store.wait()


def gram_of(factors):
    ranks, rows = factors[0].shape
    return call(
        gram_kernel,
        "gram",
        factors,
        pltpu.HBM((ranks, ranks), HALF),
        out_specs=HBM,
        scratch=[pltpu.VMEM((ranks, ranks), HALF), pltpu.SemaphoreType.DMA],
        flops=8 * rows * ranks * ranks,
    )


def spread_kernel(pieces_ref, out_ref):
    total = pieces_ref[0].astype(F32)
    for i in range(1, pieces_ref.shape[0]):
        total += pieces_ref[i].astype(F32)
    out_ref[...] = jnp.broadcast_to(total.astype(HALF)[None], out_ref.shape)


def spread(pieces):
    return call(spread_kernel, "spread", [pieces], jax.ShapeDtypeStruct(pieces.shape, HALF), flops=pieces.size)


def cross_kernel(half, adds, at_ref, *refs):
    factors, blocks = refs[:4], refs[4:8]
    extra = refs[8] if adds else None
    outs, (mixed, held, sems) = refs[8 + adds:-3], refs[-3:]
    rows = blocks[0].shape[0]
    base = pl.multiple_of(at_ref[0] * TILE, 128)
    copies = []
    for turn in range(4):
        quarter = lax.rem(at_ref[1] + turn, 4)
        for part in range(4):
            at = part * QUARTER + quarter * EIGHTH if half == 0 else quarter * QUARTER + part * EIGHTH
            to = turn * QUARTER + part * EIGHTH
            for i in range(4):
                mixed[to:to + EIGHTH, i * rows:(i + 1) * rows] = factors[i][
                    pl.ds(pl.multiple_of(at, EIGHTH), EIGHTH), :
                ]
    factor = mixed[...]
    for at in range(0, TILE, 512):
        size = min(512, TILE - at)
        block = jnp.concatenate([b[:, pl.ds(pl.multiple_of(base + at, 128), size)] for b in blocks], axis=0)
        total = jnp.dot(factor, block, preferred_element_type=F32)
        here = slice(at, at + size)
        for turn in range(4):
            value = total[turn * QUARTER:(turn + 1) * QUARTER]
            if adds:
                value = value + extra[turn, :, here].astype(F32)
            held[turn, :, here] = value.astype(HALF)
            out = outs[turn] if adds else outs[0].at[turn]
            copies.append(
                pltpu.make_async_copy(held.at[turn, :, here], out.at[:, here], sems.at[len(copies)])
            )
            copies[-1].start()
    for copy in copies:
        copy.wait()


def cross(factors, blocks, tile, half, at, extra=None):
    rows, width = blocks[0].shape
    ranks = factors[0].shape[0]
    adds = extra is not None
    if adds:
        out_shape = [pltpu.HBM((QUARTER, TILE), HALF)] * 4
    else:
        out_shape = pltpu.HBM((4, QUARTER, TILE), HALF)
    return call(
        functools.partial(cross_kernel, half, adds),
        "cross_add" if adds else "cross",
        [jnp.stack([tile, at]).astype(jnp.int32), *factors, *blocks] + ([extra] if adds else []),
        out_shape,
        in_specs=[SMEM] + [VMEM] * (8 + adds),
        out_specs=[HBM] * 4 if adds else HBM,
        scratch=[
            pltpu.VMEM((ranks, 4 * rows), HALF),
            pltpu.VMEM((4, QUARTER, TILE), HALF),
            pltpu.SemaphoreType.DMA((16,)),
        ],
        flops=8 * rows * TILE * ranks,
    )


def fold_kernel(at_ref, *refs):
    terms, outs, (taken, held, in_sems, out_sems) = refs[:8], refs[8:16], refs[16:]
    loads = [pltpu.make_async_copy(terms[i], taken.at[i], in_sems.at[i]) for i in range(8)]
    stores = [pltpu.make_async_copy(held.at[i], outs[i], out_sems.at[i]) for i in range(8)]
    for load in loads:
        load.start()
    for side in range(2):
        for load in loads[4 * side:4 * side + 4]:
            load.wait()
        for turn in range(4):
            at = lax.rem(at_ref[side] + turn, 4) * EIGHTH
            here = pl.ds(pl.multiple_of(at, EIGHTH), EIGHTH)
            total = taken[4 * side, here, :].astype(F32)
            for i in range(1, 4):
                total += taken[4 * side + i, here, :].astype(F32)
            held[4 * side + turn] = total.astype(HALF)
            stores[4 * side + turn].start()
    for store in stores:
        store.wait()


def fold(first, second, at_first, at_second):
    return call(
        fold_kernel,
        "fold",
        [jnp.stack([at_first, at_second]).astype(jnp.int32), *in_hbm([*first, *second])],
        [pltpu.HBM((EIGHTH, TILE), HALF)] * 8,
        in_specs=[SMEM] + [HBM] * 8,
        out_specs=[HBM] * 8,
        scratch=[
            pltpu.VMEM((8, QUARTER, TILE), HALF),
            pltpu.VMEM((8, EIGHTH, TILE), HALF),
            pltpu.SemaphoreType.DMA((8,)),
            pltpu.SemaphoreType.DMA((8,)),
        ],
        flops=8 * QUARTER * TILE,
    )


def finish_kernel(*refs):
    terms, out, (taken, held, in_sems, out_sem) = refs[:8], refs[8], refs[9:]
    loads = [pltpu.make_async_copy(terms[i], taken.at[i], in_sems.at[i]) for i in range(8)]
    for load in loads:
        load.start()
    for side in range(2):
        for load in loads[4 * side:4 * side + 4]:
            load.wait()
        total = taken[4 * side].astype(F32)
        for i in range(1, 4):
            total += taken[4 * side + i].astype(F32)
        held[side * EIGHTH:(side + 1) * EIGHTH, :] = total.astype(HALF)
    store = pltpu.make_async_copy(held, out, out_sem)
    store.start()
    store.wait()


def finish(first, second):
    return call(
        finish_kernel,
        "finish",
        in_hbm([*first, *second]),
        pltpu.HBM((2 * EIGHTH, TILE), HALF),
        in_specs=[HBM] * 8,
        out_specs=HBM,
        scratch=[
            pltpu.VMEM((8, EIGHTH, TILE), HALF),
            pltpu.VMEM((2 * EIGHTH, TILE), HALF),
            pltpu.SemaphoreType.DMA((8,)),
            pltpu.SemaphoreType.DMA,
        ],
        flops=8 * EIGHTH * TILE,
    )


def tile_of(total, tile):
    ranks = 16 * EIGHTH
    return total[:, tile % 2, tile // 2].reshape(ranks, TILE)


def right_kernel(rows_hbm, weights_hbm, total_hbm, raw_ref, squares_ref, weights_ref, total_ref, rows_ref, sems):
    count = raw_ref.shape[0]
    loads = [pltpu.make_async_copy(rows_hbm, rows_ref, sems.at[4])]
    for tile in range(4):
        here = (slice(None), tile % 2, tile // 2)
        loads.append(pltpu.make_async_copy(total_hbm.at[here], total_ref.at[here], sems.at[tile]))
    loads.append(pltpu.make_async_copy(weights_hbm, weights_ref, sems.at[5]))
    for load in loads:
        load.start()
    loads[0].wait()
    squares = 0.0
    for tile in range(4):
        loads[1 + tile].wait()
        both = jnp.dot(rows_ref[...], tile_of(total_ref, tile), preferred_element_type=F32)
        raw = both[:count] + both[count:]
        raw_ref[:, tile * TILE:(tile + 1) * TILE] = raw
        squares += jnp.sum(raw * raw, axis=1, keepdims=True)
    squares_ref[...] = jnp.broadcast_to(squares, squares_ref.shape)
    loads[5].wait()


def right_rows(rows, weights, total):
    count = rows.shape[0] // 2
    return call(
        right_kernel,
        "right_rows",
        in_hbm([rows, weights, total]),
        [
            jax.ShapeDtypeStruct((count, 4 * TILE), F32),
            jax.ShapeDtypeStruct((count, 128), F32),
            pltpu.VMEM(weights.shape, weights.dtype),
            pltpu.VMEM(total.shape, total.dtype),
        ],
        in_specs=[HBM] * 3,
        scratch=[pltpu.VMEM(rows.shape, rows.dtype), pltpu.SemaphoreType.DMA((6,))],
        flops=2 * rows.size * 4 * TILE,
    )


def feedback_kernel(at_ref, weights_ref, total_ref, *refs):
    blocks, out, (held, sems) = refs[:8], refs[8], refs[9:]
    rows = blocks[0].shape[0]
    ranks = 16 * EIGHTH
    copies = []
    for tile in range(4):
        for start in range(0, TILE, CHUNK):
            size = min(CHUNK, TILE - start)
            total = total_ref[:, tile % 2, tile // 2, :, start:start + size].reshape(ranks, size)
            here = (tile % 2) * TILE + start
            to = slice(tile * TILE + start, tile * TILE + start + size)
            for turn in range(4):
                part = jnp.dot(
                    weights_ref[turn * rows:(turn + 1) * rows, :], total, preferred_element_type=F32
                )
                at = lax.rem(at_ref[0] - turn + 4, 4) * rows
                held[pl.ds(pl.multiple_of(at, rows), rows), to] = (
                    blocks[4 * (tile // 2) + turn][:, here:here + size].astype(F32) - part
                ).astype(HALF)
            copies.append(pltpu.make_async_copy(held.at[:, to], out.at[:, to], sems.at[len(copies)]))
            copies[-1].start()
    for copy in copies:
        copy.wait()


def apply_feedback(weights, total, blocks, place):
    rows = blocks[0].shape[0]
    ranks = weights.shape[1]
    shape = (4 * rows, 4 * TILE)
    return call(
        feedback_kernel,
        "feedback",
        [jnp.full((1,), place, jnp.int32), weights, total, *blocks],
        pltpu.HBM(shape, HALF),
        in_specs=[SMEM] + [VMEM] * 10,
        out_specs=HBM,
        scratch=[pltpu.VMEM(shape, HALF), pltpu.SemaphoreType.DMA((4 * -(-TILE // CHUNK),))],
        flops=32 * rows * TILE * ranks,
    )


def after(value, *others):
    return lax.optimization_barrier((value,) + others)[0]


def per_device(momentum, gradient, right_factor):
    ranks_dev, width = right_factor.shape
    half_width = width // 2
    at_y, at_x, core, place = (lax.axis_index(name) for name in ("y", "x", "core", "col"))
    row = ("y", "x", "core")
    right_all = lax.all_gather(right_factor, row, axis=0, tiled=True)
    ranks = right_all.shape[0]
    blocks = [[None] * 4, [None] * 4]
    last = place
    for half in range(2):
        for turn in (2, 1, 3, 0):
            block = lax.rem(place + turn, 4) * 2 + half
            start = after(block, last) * half_width
            pair = [lax.dynamic_slice_in_dim(v, start, half_width, 1).astype(F32) for v in (momentum, gradient)]
            last = (pair[0] + pair[1]).astype(HALF)
            blocks[half][turn] = ring(last, "col", turn) if turn else last
    partial = project(blocks[0], right_all, 0)
    parts = project(blocks[1], right_all, 1, partial)
    terms = [parts[0]] + [ring(parts[turn], "col", -turn) for turn in (2, 1, 3)]
    mine, turned = settle(terms)
    factors = [turned] + [ring(turned, "col", turn) for turn in (1, 2, 3)]

    places = (at_x, at_y)
    sent = [cross(factors, blocks[half], 1 - core, half, places[half]) for half in range(2)]
    got = [swap_cores(value) for value in sent]
    first = list(cross(factors, blocks[0], after(core, sent[1]), 0, at_x, got[0]))
    second = list(cross(factors, blocks[1], after(core, first[0]), 1, at_y, got[1]))
    for turn in (2, 1, 3):
        first[turn] = ring(after(first[turn], second[0]), "x", turn)
        second[turn] = ring(second[turn], "y", turn)

    gram_part = gram_of([after(factors[0], first[2])] + factors[1:])
    rows = ranks // ranks_dev
    gram_pieces = lax.all_to_all(gram_part, row, split_axis=0, concat_axis=0, tiled=True)
    copies = spread(gram_pieces.reshape(rows, ranks_dev, ranks))

    pieces = fold(first, second, at_y, at_x)
    first, second = list(pieces[:4]), list(pieces[4:])
    for turn in (2, 1, 3):
        first[turn] = ring(first[turn], "y", turn)
    gram = lax.all_to_all(copies.reshape(ranks, ranks), row, split_axis=0, concat_axis=0, tiled=True)
    for turn in (2, 1, 3):
        second[turn] = ring(second[turn], "x", turn)
    done = finish([after(first[0], copies)] + first[1:], second)
    total = lax.all_gather(done, row, axis=0, tiled=True)
    total = total.reshape(16, 2, 2, EIGHTH, TILE)

    at_row = (at_y * 4 + at_x) * 2 + core
    own, weights, left_factor = factorize(after(gram, done), factors, at_row, ranks_dev)

    right_raw, squares, weights, total = right_rows(own, weights, total)
    squares = squares + sum(ring(squares, "col", turn) for turn in (1, 2, 3))
    new_momentum = apply_feedback(weights, total, blocks[0] + blocks[1], place)
    new_right = right_raw / jnp.sqrt(squares[:, :1] + 1e-06)
    return (new_momentum, left_factor, new_right)


def solution(mesh):
    fine = Mesh(mesh.devices.reshape(4, 4, 2, 4), ("y", "x", "core", "col"))
    every = ("y", "x", "core", "col")
    row = ("y", "x", "core")
    in_specs = (P(every, None), P(every, None), P(row, "col"))
    out_specs = (P(row, "col"), P(every, None), P(row, "col"))
    return jax.shard_map(
        per_device, mesh=fine, in_specs=in_specs, out_specs=out_specs, check_vma=False
    )
```
